512 devices in a mesh: seq: 64 (over y, x, z_lo), tensor: 8 (over z_hi, core).
Axes of the slice: x: 4, y: 8, z: 8 (z_hi: 4, z_lo: 2; z = z_hi * 2 + z_lo), core: 2. Of those that a mesh axis runs over, the one named last changes fastest.
Arguments:
- queries: bfloat16 [8192, 3072], P('seq', 'tensor'), may hold values from -12 to 12
- keys: bfloat16 [8192, 3072], P('seq', 'tensor'), may hold values from -6 to 6
- values: bfloat16 [8192, 3072], P('seq', 'tensor'), may hold values from -6 to 6
- residual: bfloat16 [8192, 6144], P('seq', 'tensor'), may hold values from -40 to 40
- out_weight: bfloat16 [3072, 6144], P('seq', 'tensor'), may hold values from -0.109375 to 0.109375
- pred_hidden: bfloat16 [2, 8192, 1024], P(None, 'seq'), may hold values from -16 to 16
- pred_weight: bfloat16 [1024, 6144], P(None, 'tensor'), may hold values from -0.1875 to 0.1875
- mask: int32 [2, 8192], P(None, 'seq'), may hold values from 0 to 1, as said below
Outputs:
- target: bfloat16 [8192, 6144], P('seq', 'tensor')
- pred_grad: float32 [1024, 6144], P('seq', 'tensor')
The draws below stay inside these ranges and needn't reach their ends.
Inputs may be any that keep to these rules, and one draw needn't show every extreme that they name: In each clip c, each mask marks the same 384 spatial positions s in every time step t, position c * 4096 + t * 512 + s; so it marks 3072 positions of each clip.
All inputs are finite; a program needn't handle non-finite values.
Results may differ from the reference program's by a relative error of at most 0.0035.
Values may be sent and summed in bfloat16 or wider, within the bound.
No kernel may reach another device: no remote copies, remote signals or barrier semaphores. Data moves between devices by JAX's collectives and lax.ppermute only.
A program may use at most 64 MiB of HBM per device.

```python
import math
import jax
import jax.numpy as jnp
from jax import lax

D = 6144
HEADS = 24
HD = 128
PW = 1024
CLIP = 4096
TIMES = 8
MASKS = 2
HQ = 3072
CLIPS = 2
TOKENS = 8192
SPATIAL = 512
SPAT_MASKED = 384
MASKED = 3072


def draw_queries(key, part):
    key = jax.random.fold_in(key, 3)
    base = jnp.clip(2.5 * jax.random.normal(key, (TOKENS, HQ), jnp.float32), -12.0, 12.0)
    return base.astype(jnp.bfloat16)


def draw_keys(key, part):
    key = jax.random.fold_in(key, 5)
    base = jnp.clip(jax.random.normal(key, (TOKENS, HQ), jnp.float32), -6.0, 6.0)
    return base.astype(jnp.bfloat16)


def draw_residual(key, part):
    key = jax.random.fold_in(key, 7)
    first, second, third = jax.random.split(key, 3)
    columns = jnp.arange(D, dtype=jnp.float32) / D
    column_scale = jnp.exp(math.log(3.0) * columns) * jnp.power(10.0, jax.random.uniform(second, (D,), jnp.float32, 0.0, 1.0))
    row_scale = jnp.power(10.0, jax.random.uniform(third, (TOKENS, 1), jnp.float32, 0.0, 0.5))
    base = jax.random.normal(first, (TOKENS, D), jnp.float32)
    return jnp.clip(0.1 * base * column_scale[None, :] * row_scale, -40.0, 40.0).astype(jnp.bfloat16)


def one_mask(key):
    first, second, third = jax.random.split(key, 3)
    starts = jax.random.randint(first, (4,), 0, SPATIAL)
    spans = jax.random.randint(second, (4,), SPATIAL // 8, SPATIAL // 3 + 1)
    places = jnp.arange(SPATIAL, dtype=jnp.int32)
    offsets = (places[None, :] - starts[:, None]) % SPATIAL
    cover = jnp.sum((offsets < spans[:, None]).astype(jnp.int32), axis=0)
    tiebreak = jax.random.permutation(third, SPATIAL).astype(jnp.int32)
    score = cover * SPATIAL + tiebreak
    order = jnp.argsort(-score, stable=True)
    ranks = jnp.zeros((SPATIAL,), jnp.int32).at[order].set(places)
    spatial_mask = (ranks < SPAT_MASKED).astype(jnp.int32)
    return jnp.tile(spatial_mask, TIMES)


def draw_mask(key, part):
    key = jax.random.fold_in(key, 11)
    masks = jax.vmap(one_mask)(jax.random.split(key, MASKS * CLIPS))
    return masks.reshape(MASKS, CLIPS * CLIP)


def strengthened(values, rng, source, target, blocks, factor):
    def block_of(axis_at):
        return (jnp.arange(values.shape[axis_at]) // (values.shape[axis_at] // blocks)).reshape((-1,) + (1,) * (values.ndim - 1 - axis_at))

    one_side = jax.random.permutation(rng, blocks)[block_of(target)]
    far = (block_of(target) + blocks // 2) % blocks
    return jnp.where((block_of(source) == one_side) | (block_of(source) == far), factor * values, values)


def levels(own_key, dims, pieces, least, high):
    factor_of, own = 1.0, jax.random.fold_in(own_key, 6)
    for position, parts in pieces:
        draws = jnp.exp(jax.random.uniform(jax.random.fold_in(own, position), (parts,), jnp.float32, least / len(pieces), high / len(pieces)))
        factor_of = factor_of * jnp.repeat(draws, dims[position] // parts).reshape([-1 if axis == position else 1 for axis in range(len(dims))])
    return factor_of


def scatter_about(stream_key, extent, deviation, most, shards=(), held_as=jnp.bfloat16):
    values = jax.random.normal(stream_key, extent, jnp.float32) * deviation
    if len(shards) > 0:
        values = levels(stream_key, extent, shards, -0.22, 0.18) * values
    return jnp.clip(values, min=-most, max=most).astype(held_as)


def noise_with(own_key, shape, spread, bound, shards, heavy, held_as=jnp.bfloat16):
    result = spread * jax.random.normal(own_key, shape, jnp.float32)
    if shards:
        result = result * levels(own_key, shape, shards, -0.22, 0.18)
    return jnp.clip(strengthened(result, jax.random.fold_in(own_key, 3), *heavy), -bound, bound).astype(held_as)


def setup_inputs(seed: int = 0) -> dict:
    key_of = jax.random.split(jax.random.key(seed), 9)
    return {
        "queries": draw_queries(jax.random.fold_in(key_of[8], 71), 0),
        "keys": draw_keys(jax.random.fold_in(key_of[8], 71), 0),
        "values": scatter_about(key_of[2], (TOKENS, HQ), 1.0, 6.0, ((0, 64), (1, 8))),
        "residual": draw_residual(jax.random.fold_in(key_of[8], 71), 0),
        "out_weight": scatter_about(key_of[4], (HQ, D), HQ ** -0.5, 0.109375, ((0, 64), (1, 8))),
        "pred_hidden": noise_with(key_of[5], (MASKS, TOKENS, PW), 1.0, 16.0, ((1, 64),), (1, 2, 64, 4.0)),
        "pred_weight": scatter_about(key_of[6], (PW, D), PW ** -0.5, 0.1875, ((1, 8),)),
        "mask": draw_mask(jax.random.fold_in(key_of[8], 71), 0),
    }


def one_head(operands):
    query_head, key_head, value_head = operands
    scores = jnp.dot(query_head, key_head.T, preferred_element_type=jnp.float32) / math.sqrt(HD)
    largest = lax.optimization_barrier(jnp.max(scores, axis=1, keepdims=True))
    exponent = jnp.exp(scores - largest)
    totals = lax.optimization_barrier(jnp.sum(exponent, axis=1, keepdims=True))
    weights = exponent.astype(jnp.bfloat16)
    return (jnp.dot(weights, value_head, preferred_element_type=jnp.float32) / totals).astype(jnp.bfloat16)

def reference(queries, keys, values, residual, out_weight, pred_hidden, pred_weight, mask):

    def split_heads(array):
        return array.reshape(CLIPS, CLIP, HEADS, HD).transpose(0, 2, 1, 3).reshape(CLIPS * HEADS, CLIP, HD)
    attended = lax.map(one_head, (split_heads(queries), split_heads(keys), split_heads(values)))
    attended = attended.reshape(CLIPS, HEADS, CLIP, HD).transpose(0, 2, 1, 3).reshape(TOKENS, HQ)
    projected = jnp.dot(attended, out_weight, preferred_element_type=jnp.float32)
    summed = residual.astype(jnp.float32) + projected
    mean = lax.optimization_barrier(jnp.mean(summed, axis=1, keepdims=True))
    centered = summed - mean
    var = lax.optimization_barrier(jnp.mean(centered * centered, axis=1, keepdims=True))
    target = (centered * lax.rsqrt(var + 1e-06)).astype(jnp.bfloat16)
    target_wide = target.astype(jnp.float32)

    def add_mask(total, operands):
        hidden_rows, mask_row = operands
        pred = jnp.dot(hidden_rows, pred_weight, preferred_element_type=jnp.float32)
        error = (jnp.clip(pred - target_wide, -1.0, 1.0) * mask_row.astype(jnp.float32)[:, None]).astype(jnp.bfloat16)
        return (total + jnp.dot(hidden_rows.T, error, preferred_element_type=jnp.float32), None)
    summed_grad, unused = lax.scan(add_mask, jnp.zeros((PW, D), jnp.float32), (pred_hidden, mask))
    pred_grad = summed_grad / math.sqrt(MASKS * CLIPS * MASKED)
    return (target, pred_grad)
```

```python
import functools
import math

import jax
import jax.numpy as jnp
from jax import lax
from jax.experimental import pallas as pl
from jax.experimental.pallas import tpu as pltpu
from jax.sharding import Mesh
from jax.sharding import PartitionSpec as P

D = 6144
HD = 128
CLIP = 4096
MASKS = 2
MASKED = 3072
HEADS_HERE = 3
SEQ = ("h", "y", "x", "z")
TENSOR = ("w", "c")
LOG2E_ROOT = math.log2(math.e) / math.sqrt(HD)


def ring(size, distance):
    return [(source, (source + distance) % size) for source in range(size)]


def column_to_row(column):
    size = column.shape[0]
    rows = lax.broadcasted_iota(jnp.int32, (size, size), 0)
    cols = lax.broadcasted_iota(jnp.int32, (size, size), 1)
    return jnp.sum(jnp.where(rows == cols, column, 0.0), axis=0, keepdims=True)


def row_to_column(row):
    size = row.shape[1]
    rows = lax.broadcasted_iota(jnp.int32, (size, size), 0)
    cols = lax.broadcasted_iota(jnp.int32, (size, size), 1)
    return jnp.sum(jnp.where(rows == cols, row, 0.0), axis=1, keepdims=True)


def attend_kernel(q_own, q_far, kv0, kv1, kv2, kv3, own, far):
    parts = (kv0, kv1, kv2, kv3)
    keys = jnp.concatenate([p[i, 0] for p in parts for i in range(p.shape[0])], axis=0)
    values = jnp.concatenate([p[i, 1] for p in parts for i in range(p.shape[0])], axis=0)
    for q_ref, out in ((q_own, own), (q_far, far)):
        count = q_ref.shape[0]
        out[count * HD :, :] = jnp.zeros((8, HD), jnp.float32)
        for block in range(0, count, 2):
            query = jnp.concatenate([q_ref[block], q_ref[block + 1]], axis=0)
            scores = lax.dot_general(
                query, keys, (((1,), (1,)), ((), ())), preferred_element_type=jnp.float32
            )
            best = jnp.max(scores, axis=1, keepdims=True)
            exponent = jnp.exp2((scores - best) * LOG2E_ROOT)
            total = jnp.sum(exponent, axis=1, keepdims=True)
            summed = jnp.dot(
                exponent.astype(jnp.bfloat16), values, preferred_element_type=jnp.float32
            )
            out[block * HD : (block + 2) * HD, :] = summed / total
            level = best * LOG2E_ROOT + jnp.log2(total)
            out[count * HD + block : count * HD + block + 1, :] = column_to_row(level[:HD])
            out[count * HD + block + 1 : count * HD + block + 2, :] = column_to_row(level[HD:])


def combine_kernel(one, two, out):
    count = out.shape[0] // HD
    for block in range(count):
        level_one = row_to_column(one[count * HD + block : count * HD + block + 1, :])
        level_two = row_to_column(two[count * HD + block : count * HD + block + 1, :])
        best = jnp.maximum(level_one, level_two)
        weight_one = jnp.exp2(level_one - best)
        weight_two = jnp.exp2(level_two - best)
        rows = slice(block * HD, (block + 1) * HD)
        out[rows, :] = (
            (weight_one * one[rows, :] + weight_two * two[rows, :]) / (weight_one + weight_two)
        ).astype(jnp.bfloat16)


VMEM = pl.BlockSpec(memory_space=pltpu.VMEM)


def attend(q_own, q_far, kvs):
    rows = q_own.shape[0] * HD + 8
    shape = jax.ShapeDtypeStruct((rows, HD), jnp.float32)
    return pl.pallas_call(
        attend_kernel,
        out_shape=(shape, shape),
        in_specs=[VMEM] * 6,
        out_specs=(VMEM, VMEM),
        compiler_params=pltpu.CompilerParams(vmem_limit_bytes=40 * 1024 * 1024),
        cost_estimate=pl.CostEstimate(
            flops=4 * 1024 * 2048 * HD, bytes_accessed=2**21, transcendentals=1024 * 2048
        ),
    )(q_own, q_far, *kvs)


def combine(one, two):
    return pl.pallas_call(
        combine_kernel,
        out_shape=jax.ShapeDtypeStruct((one.shape[0] - 8, HD), jnp.bfloat16),
        in_specs=[VMEM] * 2,
        out_specs=VMEM,
    )(one, two)


def by_head(array):
    tokens = array.shape[0]
    heads = array.reshape(tokens, HEADS_HERE, HD).transpose(1, 0, 2)
    return jnp.concatenate([heads, heads[2:]], axis=0)


def body(queries, keys, values, residual, out_weight, pred_hidden, pred_weight, mask):
    tokens_here = queries.shape[0]
    packed = jnp.stack((by_head(keys), by_head(values), by_head(queries)), axis=1)
    packed = lax.all_to_all(packed, "y", 0, 0, tiled=True)
    kv_own = packed[:, :2]
    q_own = packed[:, 2]
    kvs = [kv_own] + [lax.ppermute(kv_own, "x", ring(4, d)) for d in (2, 1, 3)]
    q_far = lax.ppermute(q_own, "z", ring(2, 1))

    weight_rows = lax.all_gather(out_weight, "z", axis=0, tiled=True)
    weight_rows = lax.all_gather(weight_rows, "x", axis=0, tiled=True)
    weight_heads = weight_rows.reshape(HEADS_HERE, HD, -1)
    weight_heads = jnp.concatenate([weight_heads, weight_heads[2:]], axis=0)
    weight_heads = jnp.concatenate([weight_heads, weight_heads], axis=0)
    weight_here = lax.all_to_all(weight_heads, ("h", "y"), 0, 0, tiled=True)

    own, far = attend(q_own, q_far, kvs)
    arrived = lax.ppermute(far, "z", ring(2, 1))
    attended = combine(own, arrived)

    every = lax.all_gather(attended, "w", axis=0)
    every = lax.all_gather(every, "c", axis=1)
    columns = every.reshape(8, 4 * tokens_here, HD).transpose(1, 0, 2).reshape(4 * tokens_here, 8 * HD)
    part = jnp.dot(
        columns, weight_here.reshape(8 * HD, -1), preferred_element_type=jnp.float32
    )
    part = part.astype(jnp.bfloat16).reshape(4, tokens_here, -1)
    part = lax.all_to_all(part, "y", 0, 0, tiled=True)
    projected = (
        part[0].astype(jnp.float32) + part[1].astype(jnp.float32) + part[2].astype(jnp.float32)
    )
    summed = residual.astype(jnp.float32) + projected

    width = summed.shape[1]
    mean_here = jnp.sum(summed, axis=1) / width
    off = summed - mean_here[:, None]
    square_here = jnp.sum(off * off, axis=1)
    both = lax.all_gather(jnp.stack((mean_here, square_here)), TENSOR, axis=0)
    mean = jnp.sum(both[:, 0], axis=0) * (width / D)
    shift = both[:, 0] - mean[None, :]
    var = jnp.sum(both[:, 1] + width * shift * shift, axis=0) / D
    target = ((summed - mean[:, None]) * lax.rsqrt(var + 1e-06)[:, None]).astype(jnp.bfloat16)

    mask_count, tokens_pred, width_pred = pred_hidden.shape
    clip_total = 2
    flat_hidden = pred_hidden.reshape(mask_count * tokens_pred, width_pred)
    pred = jnp.dot(flat_hidden, pred_weight, preferred_element_type=jnp.float32).reshape(
        mask_count, tokens_pred, width
    )
    difference = pred - target.astype(jnp.float32)[None, :, :]
    error = (jnp.clip(difference, -1.0, 1.0) * mask.astype(jnp.float32)[:, :, None]).astype(
        jnp.bfloat16
    )
    error = error.reshape(mask_count * tokens_pred, width)
    grad_scale = 1.0 / math.sqrt(MASKS * clip_total * MASKED)
    product = lax.dot_general(
        flat_hidden, error, (((0,), (0,)), ((), ())), preferred_element_type=jnp.float32
    )
    product = product.astype(jnp.bfloat16).reshape(64, -1, width)
    product = lax.all_to_all(product, SEQ, 0, 0, tiled=True)
    pred_grad = jnp.sum(product.astype(jnp.float32), axis=0) * grad_scale
    return (target, pred_grad)


def solution(mesh):
    fine = Mesh(mesh.devices.reshape(2, 4, 4, 2, 4, 2), SEQ + TENSOR)
    placed = (
        P(SEQ, TENSOR),
        P(SEQ, TENSOR),
        P(SEQ, TENSOR),
        P(SEQ, TENSOR),
        P(SEQ, TENSOR),
        P(None, SEQ, None),
        P(None, TENSOR),
        P(None, SEQ),
    )
    return jax.shard_map(
        body,
        mesh=fine,
        in_specs=placed,
        out_specs=(P(SEQ, TENSOR), P(SEQ, TENSOR)),
        check_vma=False,
    )
```

```python
import math

import jax
import jax.numpy as jnp
from jax import lax
from jax.experimental import pallas as pl
from jax.experimental.pallas import tpu as pltpu
from jax.sharding import Mesh
from jax.sharding import PartitionSpec as P

D = 6144
HD = 128
CLIPS = 2
MASKS = 2
MASKED = 3072
HEADS_HERE = 3
SEQ = ("h", "y", "x", "z")
TENSOR = ("w", "c")
LOG2E_ROOT = math.log2(math.e) / math.sqrt(HD)
LEVEL_ROWS = 16
VMEM = pl.BlockSpec(memory_space=pltpu.VMEM)
SMEM = pl.BlockSpec(memory_space=pltpu.SMEM)
ROOMY = pltpu.CompilerParams(vmem_limit_bytes=40 * 1024 * 1024)


def ring(size, distance):
    return [(source, (source + distance) % size) for source in range(size)]


def diagonal(size):
    rows = lax.broadcasted_iota(jnp.int32, (size, size), 0)
    return rows == lax.broadcasted_iota(jnp.int32, (size, size), 1)


def column_to_row(column):
    return jnp.sum(jnp.where(diagonal(column.shape[0]), column, 0.0), axis=0, keepdims=True)


def row_to_column(row):
    return jnp.sum(jnp.where(diagonal(row.shape[1]), row, 0.0), axis=1, keepdims=True)


def pack_kernel(queries, keys, values, out):
    for place in range(4):
        head = min(place, HEADS_HERE - 1)
        columns = slice(head * HD, (head + 1) * HD)
        out[place, 0] = keys[:, columns]
        out[place, 1] = values[:, columns]
        out[place, 2] = queries[:, columns]


def pack(queries, keys, values):
    tokens = queries.shape[0]
    return pl.pallas_call(
        pack_kernel,
        out_shape=jax.ShapeDtypeStruct((4, 3, tokens, HD), jnp.bfloat16),
        in_specs=[VMEM] * 3,
        out_specs=VMEM,
    )(queries, keys, values)


def attend_kernel(here, q_own, q_far, kv0, kv1, kv2, kv3, out):
    parts = (kv0, kv1, kv2, kv3)
    keys = jnp.concatenate([p[i, 0] for p in parts for i in range(p.shape[0])], axis=0)
    values = jnp.concatenate([p[i, 1] for p in parts for i in range(p.shape[0])], axis=0)
    for q_ref, place in ((q_own, here[0]), (q_far, 1 - here[0])):
        for block in range(0, q_ref.shape[0], 2):
            query = jnp.concatenate([q_ref[block], q_ref[block + 1]], axis=0)
            scores = lax.dot_general(
                query, keys, (((1,), (1,)), ((), ())), preferred_element_type=jnp.float32
            )
            best = jnp.max(scores, axis=1, keepdims=True)
            exponent = jnp.exp2((scores - best) * LOG2E_ROOT)
            total = jnp.sum(exponent, axis=1, keepdims=True)
            summed = jnp.dot(
                exponent.astype(jnp.bfloat16), values, preferred_element_type=jnp.float32
            )
            summed = (summed / total).astype(jnp.bfloat16)
            level = best * LOG2E_ROOT + jnp.log2(total)
            for half in range(2):
                rows = slice(half * HD, (half + 1) * HD)
                row = column_to_row(level[rows])
                first = row.astype(jnp.bfloat16).astype(jnp.float32)
                second = (row - first).astype(jnp.bfloat16).astype(jnp.float32)
                third = row - first - second
                terms = jnp.concatenate(
                    [first, second, third, jnp.zeros((LEVEL_ROWS - 3, HD), jnp.float32)], axis=0
                )
                chunk = 2 * (block + half) + place
                out[chunk, :HD, :] = summed[rows]
                out[chunk, HD:, :] = terms.astype(jnp.bfloat16)


def attend(here, q_own, q_far, kvs):
    chunks = 2 * q_own.shape[0]
    return pl.pallas_call(
        attend_kernel,
        out_shape=jax.ShapeDtypeStruct((chunks, HD + LEVEL_ROWS, HD), jnp.bfloat16),
        in_specs=[SMEM] + [VMEM] * 6,
        out_specs=VMEM,
        compiler_params=ROOMY,
        cost_estimate=pl.CostEstimate(
            flops=4 * 1024 * 2048 * HD, bytes_accessed=2**21, transcendentals=1024 * 2048
        ),
    )(here, q_own, q_far, *kvs)


def combine_kernel(chunks, out):
    for head in range(HEADS_HERE):
        levels = []
        for part in range(2):
            terms = chunks[2 * head + part, HD:, :].astype(jnp.float32)
            levels.append(row_to_column(terms[0:1] + terms[1:2] + terms[2:3]))
        best = jnp.maximum(levels[0], levels[1])
        weights = [jnp.exp2(level - best) for level in levels]
        summed = sum(
            weights[part] * chunks[2 * head + part, :HD, :].astype(jnp.float32) for part in range(2)
        )
        out[:, head * HD : (head + 1) * HD] = (summed / (weights[0] + weights[1])).astype(
            jnp.bfloat16
        )


def combine(chunks):
    return pl.pallas_call(
        combine_kernel,
        out_shape=jax.ShapeDtypeStruct((HD, HEADS_HERE * HD), jnp.bfloat16),
        in_specs=[VMEM],
        out_specs=VMEM,
    )(chunks)


def project_kernel(columns, weight, residual, summed, stats, total):
    step = pl.program_id(0)
    product = jnp.dot(columns[0], weight[...], preferred_element_type=jnp.float32)

    @pl.when(step == 0)
    def _():
        total[...] = residual[...].astype(jnp.float32) + product

    @pl.when(step > 0)
    def _():
        total[...] += product

    @pl.when(step == pl.num_programs(0) - 1)
    def _():
        value = total[...]
        summed[...] = value
        mean = jnp.sum(value, axis=1, keepdims=True) / value.shape[1]
        off = value - mean
        stats[0:1, :] = column_to_row(mean)
        stats[1:2, :] = column_to_row(jnp.sum(off * off, axis=1, keepdims=True))


def project(columns, weight, residual):
    pieces, tokens, depth = columns.shape
    width = weight.shape[1]
    return pl.pallas_call(
        project_kernel,
        grid=(pieces,),
        out_shape=(
            jax.ShapeDtypeStruct((tokens, width), jnp.float32),
            jax.ShapeDtypeStruct((2, tokens), jnp.float32),
        ),
        in_specs=[
            pl.BlockSpec((1, tokens, depth), lambda i: (i, 0, 0)),
            pl.BlockSpec((depth, width), lambda i: (i, 0)),
            pl.BlockSpec((tokens, width), lambda i: (0, 0)),
        ],
        out_specs=(
            pl.BlockSpec((tokens, width), lambda i: (0, 0)),
            pl.BlockSpec((2, tokens), lambda i: (0, 0)),
        ),
        scratch_shapes=[pltpu.VMEM((tokens, width), jnp.float32)],
        compiler_params=ROOMY,
        cost_estimate=pl.CostEstimate(
            flops=2 * tokens * depth * pieces * width,
            bytes_accessed=2 * depth * pieces * width,
            transcendentals=0,
        ),
    )(columns, weight, residual)


def finish_kernel(stats, summed, pred, hidden, mask, target, product):
    width = summed.shape[1]
    tokens = summed.shape[0]
    means = stats[:, 0, :]
    mean = jnp.sum(means, axis=0, keepdims=True) * (width / D)
    shift = means - mean
    var = jnp.sum(stats[:, 1, :] + width * shift * shift, axis=0, keepdims=True) / D
    scale = row_to_column(lax.rsqrt(var + 1e-06))
    value = ((summed[...] - row_to_column(mean)) * scale).astype(jnp.bfloat16)
    target[...] = value
    value = value.astype(jnp.float32)
    errors = []
    for k in range(MASKS):
        rows = slice(k * tokens, (k + 1) * tokens)
        marked = row_to_column(mask[k : k + 1, :].astype(jnp.float32))
        errors.append((jnp.clip(pred[rows, :] - value, -1.0, 1.0) * marked).astype(jnp.bfloat16))
    error = jnp.concatenate(errors, axis=0)
    step = 256
    for start in range(0, hidden.shape[0], step):
        product[start : start + step, :] = jnp.dot(
            hidden[start : start + step, :], error, preferred_element_type=jnp.float32
        ).astype(jnp.bfloat16)


def finish(stats, summed, pred, hidden, mask):
    tokens, width = summed.shape
    return pl.pallas_call(
        finish_kernel,
        out_shape=(
            jax.ShapeDtypeStruct((tokens, width), jnp.bfloat16),
            jax.ShapeDtypeStruct((hidden.shape[0], width), jnp.bfloat16),
        ),
        in_specs=[VMEM] * 5,
        out_specs=(VMEM, VMEM),
        compiler_params=ROOMY,
        cost_estimate=pl.CostEstimate(
            flops=2 * hidden.shape[0] * hidden.shape[1] * width,
            bytes_accessed=2**22,
            transcendentals=0,
        ),
    )(stats, summed, pred, hidden, mask)


def body(queries, keys, values, residual, out_weight, pred_hidden, pred_weight, mask):
    rows, width = out_weight.shape
    weight = jnp.broadcast_to(out_weight[None], (8, rows, width)).reshape(8 * rows, width)
    weight = lax.all_to_all(weight, ("x", "z"), 0, 0, tiled=True)
    weight = lax.all_gather(weight, ("h", "y"), axis=0, tiled=True)

    packed = lax.all_to_all(pack(queries, keys, values), "y", 0, 0, tiled=True)
    kv_own = packed[:, :2]
    q_own = packed[:, 2]
    kvs = [kv_own] + [lax.ppermute(kv_own, "x", ring(4, d)) for d in (2, 1, 3)]
    q_far = lax.ppermute(q_own, "z", ring(2, 1))

    flat_hidden = pred_hidden.reshape(-1, pred_hidden.shape[2])
    pred = jnp.dot(flat_hidden, pred_weight, preferred_element_type=jnp.float32)
    hidden_rows = flat_hidden.T.reshape(8, 8, -1, flat_hidden.shape[0])
    hidden_rows = hidden_rows.transpose(1, 0, 2, 3).reshape(-1, flat_hidden.shape[0])

    here = lax.axis_index("z").astype(jnp.int32).reshape(1)
    parts = attend(here, q_own, q_far, kvs)
    parts = lax.all_to_all(parts, ("y", "z"), 0, 0, tiled=True)
    attended = lax.all_gather(combine(parts), TENSOR, axis=0)

    summed, stats = project(attended, weight, residual)
    stats = lax.all_gather(stats, TENSOR, axis=0)
    target, product = finish(stats, summed, pred, hidden_rows, mask)

    product = lax.all_to_all(product.reshape(8, -1, width), ("x", "z"), 0, 0, tiled=True)
    product = jnp.sum(product.astype(jnp.float32), axis=0).astype(jnp.bfloat16)
    product = lax.all_to_all(product.reshape(8, -1, width), ("h", "y"), 0, 0, tiled=True)
    grad_scale = 1.0 / math.sqrt(MASKS * CLIPS * MASKED)
    pred_grad = jnp.sum(product.astype(jnp.float32), axis=0) * grad_scale
    return (target, pred_grad)


def solution(mesh):
    fine = Mesh(mesh.devices.reshape(2, 4, 4, 2, 4, 2), SEQ + TENSOR)
    placed = (
        P(SEQ, TENSOR),
        P(SEQ, TENSOR),
        P(SEQ, TENSOR),
        P(SEQ, TENSOR),
        P(SEQ, TENSOR),
        P(None, SEQ, None),
        P(None, TENSOR),
        P(None, SEQ),
    )
    return jax.shard_map(
        body,
        mesh=fine,
        in_specs=placed,
        out_specs=(P(SEQ, TENSOR), P(SEQ, TENSOR)),
        check_vma=False,
    )
```

```python
import math

import jax
import jax.numpy as jnp
from jax import lax
from jax.experimental import pallas as pl
from jax.experimental.pallas import tpu as pltpu
from jax.sharding import Mesh
from jax.sharding import PartitionSpec as P

D = 6144
HD = 128
CLIPS = 2
MASKS = 2
MASKED = 3072
HEADS_HERE = 3
SEQ = ("h", "y", "x", "z")
TENSOR = ("w", "c")
LOG2E_ROOT = math.log2(math.e) / math.sqrt(HD)
LEVEL_ROWS = 16
MARK_ROWS = 16
VMEM = pl.BlockSpec(memory_space=pltpu.VMEM)
SMEM = pl.BlockSpec(memory_space=pltpu.SMEM)
ROOMY = pltpu.CompilerParams(vmem_limit_bytes=40 * 1024 * 1024)


def ring(size, distance):
    return [(source, (source + distance) % size) for source in range(size)]


def neighbour(array):
    return lax.ppermute(array, "z", ring(2, 1))


def diagonal(size):
    rows = lax.broadcasted_iota(jnp.int32, (size, size), 0)
    return rows == lax.broadcasted_iota(jnp.int32, (size, size), 1)


def column_to_row(column):
    return jnp.sum(jnp.where(diagonal(column.shape[0]), column, 0.0), axis=0, keepdims=True)


def row_to_column(row):
    return jnp.sum(jnp.where(diagonal(row.shape[1]), row, 0.0), axis=1, keepdims=True)


def pack_kernel(place, queries, keys, values, weight, one, two, three, four, weights):
    for distance, out in enumerate((one, two, three, four)):
        head = jnp.minimum(place[1] ^ distance, HEADS_HERE - 1)
        columns = pl.ds(pl.multiple_of(head * HD, HD), HD)
        out[0] = keys[:, columns]
        out[1] = values[:, columns]
        out[2] = queries[:, columns]
    for copy in range(weights.shape[0]):
        weights[copy] = weight[...]


def pack(place, queries, keys, values, weight):
    piece = jax.ShapeDtypeStruct((3, queries.shape[0], HD), jnp.bfloat16)
    return pl.pallas_call(
        pack_kernel,
        out_shape=(piece,) * 4 + (jax.ShapeDtypeStruct((8,) + weight.shape, jnp.bfloat16),),
        in_specs=[SMEM] + [VMEM] * 4,
        out_specs=(VMEM,) * 5,
    )(place, queries, keys, values, weight)


def attend_kernel(place, q_own, q_far, kv0, kv1, kv2, kv3, out):
    parts = (kv0, kv1, kv2, kv3)
    keys = jnp.concatenate([p[i, 0] for p in parts for i in range(p.shape[0])], axis=0)
    values = jnp.concatenate([p[i, 1] for p in parts for i in range(p.shape[0])], axis=0)
    for q_ref, side in ((q_own, place[0]), (q_far, 1 - place[0])):
        for block in range(0, q_ref.shape[0], 2):
            query = jnp.concatenate([q_ref[block], q_ref[block + 1]], axis=0)
            scores = lax.dot_general(
                query, keys, (((1,), (1,)), ((), ())), preferred_element_type=jnp.float32
            )
            best = jnp.max(scores, axis=1, keepdims=True)
            exponent = jnp.exp2((scores - best) * LOG2E_ROOT)
            total = jnp.sum(exponent, axis=1, keepdims=True)
            summed = jnp.dot(
                exponent.astype(jnp.bfloat16), values, preferred_element_type=jnp.float32
            )
            summed = (summed / total).astype(jnp.bfloat16)
            level = best * LOG2E_ROOT + jnp.log2(total)
            for half in range(2):
                rows = slice(half * HD, (half + 1) * HD)
                row = column_to_row(level[rows])
                first = row.astype(jnp.bfloat16).astype(jnp.float32)
                second = (row - first).astype(jnp.bfloat16).astype(jnp.float32)
                third = row - first - second
                terms = jnp.concatenate(
                    [first, second, third, jnp.zeros((LEVEL_ROWS - 3, HD), jnp.float32)], axis=0
                )
                chunk = 2 * (place[1] ^ (block + half)) + side
                out[chunk, :HD, :] = summed[rows]
                out[chunk, HD:, :] = terms.astype(jnp.bfloat16)


def attend(place, q_own, q_far, kvs):
    chunks = 2 * q_own.shape[0]
    return pl.pallas_call(
        attend_kernel,
        out_shape=jax.ShapeDtypeStruct((chunks, HD + LEVEL_ROWS, HD), jnp.bfloat16),
        in_specs=[SMEM] + [VMEM] * 6,
        out_specs=VMEM,
        compiler_params=ROOMY,
        cost_estimate=pl.CostEstimate(
            flops=4 * 1024 * 2048 * HD, bytes_accessed=2**21, transcendentals=1024 * 2048
        ),
    )(place, q_own, q_far, *kvs)


def combine_kernel(place, chunks, kept, sent):
    heads = []
    for head in range(HEADS_HERE):
        levels = []
        for part in range(2):
            terms = chunks[2 * head + part, HD:, :].astype(jnp.float32)
            levels.append(row_to_column(terms[0:1] + terms[1:2] + terms[2:3]))
        best = jnp.maximum(levels[0], levels[1])
        weights = [jnp.exp2(level - best) for level in levels]
        summed = sum(
            weights[part] * chunks[2 * head + part, :HD, :].astype(jnp.float32) for part in range(2)
        )
        heads.append(summed / (weights[0] + weights[1]))
    columns = jnp.concatenate(heads, axis=1)
    halves = []
    for z in range(2):
        blocks = [columns[:, 96 * x + 48 * z : 96 * x + 48 * z + 48] for x in range(4)]
        half = None
        for x in range(4):
            turned = jnp.concatenate(blocks[x:] + blocks[:x], axis=1)
            half = turned if half is None else jnp.where(place[2] == x, turned, half)
        halves.append(half)
    first = place[0] == 0
    kept[...] = jnp.where(first, halves[0], halves[1]).astype(jnp.bfloat16)
    sent[...] = jnp.where(first, halves[1], halves[0]).astype(jnp.bfloat16)


def combine(place, chunks):
    shape = jax.ShapeDtypeStruct((HD, HEADS_HERE * HD // 2), jnp.bfloat16)
    return pl.pallas_call(
        combine_kernel,
        out_shape=(shape, shape),
        in_specs=[SMEM, VMEM],
        out_specs=(VMEM, VMEM),
    )(place, chunks)


def project_kernel(columns, residual, mask, one, two, three, four, partial, sent):
    pieces, tokens, width = columns.shape
    half = width // 2
    total = jnp.concatenate([residual[...].astype(jnp.float32), jnp.zeros(residual.shape, jnp.float32)], axis=0)
    for piece in range(pieces):
        left = jnp.concatenate([columns[piece, :, :half], columns[piece, :, half:]], axis=0)
        right = jnp.concatenate([ref[piece] for ref in (one, two, three, four)], axis=0)
        total += jnp.dot(left, right, preferred_element_type=jnp.float32)
    partial[...] = total
    sent[: 2 * tokens, :] = total.astype(jnp.bfloat16)
    marks = mask[...].astype(jnp.float32)
    marks = jnp.concatenate([marks, jnp.zeros((sent.shape[0] - 2 * tokens - MASKS, tokens), jnp.float32)], axis=0)
    sent[2 * tokens :, :] = jnp.concatenate([marks] * (sent.shape[1] // tokens), axis=1).astype(jnp.bfloat16)


def project(columns, residual, mask, weights):
    pieces, tokens, _ = columns.shape
    rows, width = weights[0].shape[1:]
    count = 4 * pieces * rows * width
    return pl.pallas_call(
        project_kernel,
        out_shape=(
            jax.ShapeDtypeStruct((2 * tokens, width), jnp.float32),
            jax.ShapeDtypeStruct((2 * tokens + MARK_ROWS, width), jnp.bfloat16),
        ),
        in_specs=[VMEM] * 7,
        out_specs=(VMEM, VMEM),
        compiler_params=ROOMY,
        cost_estimate=pl.CostEstimate(
            flops=4 * tokens * count, bytes_accessed=2 * count, transcendentals=0
        ),
    )(columns, residual, mask, *weights)


def add_kernel(partial, arrived, summed, stats):
    tokens = partial.shape[0] // 2
    for side in range(2):
        rows = slice(side * tokens, (side + 1) * tokens)
        other = slice((1 - side) * tokens, (2 - side) * tokens)
        total = partial[rows, :] + arrived[other, :].astype(jnp.float32)
        summed[rows, :] = total
        mean = jnp.sum(total, axis=1, keepdims=True) / total.shape[1]
        off = total - mean
        stats[0:1, rows] = column_to_row(mean)
        stats[1:2, rows] = column_to_row(jnp.sum(off * off, axis=1, keepdims=True))


def add_up(partial, arrived):
    rows, width = partial.shape
    return pl.pallas_call(
        add_kernel,
        out_shape=(
            jax.ShapeDtypeStruct((rows, width), jnp.float32),
            jax.ShapeDtypeStruct((2, rows), jnp.float32),
        ),
        in_specs=[VMEM] * 2,
        out_specs=(VMEM, VMEM),
        compiler_params=ROOMY,
    )(partial, arrived)


def finish_kernel(stats, summed, arrived, mask, pred, pred_far, hidden, target, product):
    rows_here, width = summed.shape
    tokens = rows_here // 2
    errors = []
    for side, prediction in enumerate((pred, pred_far)):
        rows = slice(side * tokens, (side + 1) * tokens)
        means = stats[:, 0, rows]
        mean = jnp.sum(means, axis=0, keepdims=True) * (width / D)
        shift = means - mean
        var = jnp.sum(stats[:, 1, rows] + width * shift * shift, axis=0, keepdims=True) / D
        scale = row_to_column(lax.rsqrt(var + 1e-06))
        value = ((summed[rows, :] - row_to_column(mean)) * scale).astype(jnp.bfloat16)
        if side == 0:
            target[...] = value
        value = value.astype(jnp.float32)
        for k in range(MASKS):
            if side == 0:
                marks = mask[k : k + 1, :].astype(jnp.float32)
            else:
                marks = arrived[rows_here + k : rows_here + k + 1, :tokens].astype(jnp.float32)
            difference = jnp.clip(prediction[k * tokens : (k + 1) * tokens, :] - value, -1.0, 1.0)
            errors.append((difference * row_to_column(marks)).astype(jnp.bfloat16))
    error = jnp.concatenate(errors, axis=0)
    step = 256
    for start in range(0, hidden.shape[0], step):
        product[start : start + step, :] = jnp.dot(
            hidden[start : start + step, :], error, preferred_element_type=jnp.float32
        ).astype(jnp.bfloat16)


def finish(stats, summed, arrived, mask, pred, pred_far, hidden):
    rows, width = summed.shape
    return pl.pallas_call(
        finish_kernel,
        out_shape=(
            jax.ShapeDtypeStruct((rows // 2, width), jnp.bfloat16),
            jax.ShapeDtypeStruct((hidden.shape[0], width), jnp.bfloat16),
        ),
        in_specs=[VMEM] * 7,
        out_specs=(VMEM, VMEM),
        compiler_params=ROOMY,
        cost_estimate=pl.CostEstimate(
            flops=2 * hidden.shape[0] * hidden.shape[1] * width,
            bytes_accessed=2**22,
            transcendentals=0,
        ),
    )(stats, summed, arrived, mask, pred, pred_far, hidden)


def body(queries, keys, values, residual, out_weight, pred_hidden, pred_weight, mask):
    place = jnp.stack(
        [lax.axis_index(name) for name in ("z", "y", "x")]
    ).astype(jnp.int32)
    *pieces, weight = pack(place, queries, keys, values, out_weight)
    for distance in (1, 2, 3):
        pairs = [(i, i ^ distance) for i in range(4) if i ^ distance < HEADS_HERE]
        pieces[distance] = lax.ppermute(pieces[distance], "y", pairs)
    pieces[1], weight = lax.optimization_barrier((pieces[1], weight))
    kv_own = jnp.stack([piece[:2] for piece in pieces])
    q_own = jnp.stack([piece[2] for piece in pieces])

    width = out_weight.shape[1]
    weight = lax.all_to_all(weight, ("h", "y"), 0, 0, tiled=True)

    kvs = [kv_own] + [lax.ppermute(kv_own, "x", ring(4, d)) for d in (2, 1, 3)]
    q_far = neighbour(q_own)
    kvs, q_far, weight = lax.optimization_barrier((kvs, q_far, weight))
    parts = attend(place, q_own, q_far, kvs)

    hidden = pred_hidden.reshape(-1, pred_hidden.shape[2])
    hidden_far = neighbour(hidden)

    def predict(states):
        return jnp.dot(states, pred_weight, preferred_element_type=jnp.float32)

    hidden_own, parts = lax.optimization_barrier((hidden, parts))
    pred = predict(hidden_own)
    weight, pred = lax.optimization_barrier((weight, pred))
    weights = [weight] + [lax.ppermute(weight, "x", ring(4, -d)) for d in (1, 2, 3)]

    parts = lax.all_to_all(parts, ("y", "z"), 0, 0, tiled=True)
    parts, hidden_far = lax.optimization_barrier((parts, hidden_far))
    kept, sent = combine(place, parts)
    attended = jnp.concatenate((kept, neighbour(sent)), axis=1)
    attended = lax.all_gather(attended, "w", axis=0)
    attended = lax.all_gather(attended, "c", axis=1).reshape((8,) + attended.shape[1:])

    partial, sent = project(attended, residual, mask, weights)
    arrived = neighbour(sent)
    hidden, hidden_far, sent = lax.optimization_barrier((hidden, hidden_far, sent))
    pred_far = predict(hidden_far)
    z = lax.axis_index("z")
    hidden_rows = [
        lax.dynamic_index_in_dim(h.T.reshape(8, 4, 2, 16, -1), z, 2, keepdims=False)
        for h in (hidden, hidden_far)
    ]
    hidden_rows = jnp.concatenate(hidden_rows, axis=3).transpose(1, 0, 2, 3)
    hidden_rows = hidden_rows.reshape(-1, 2 * hidden.shape[0])

    summed, stats = add_up(partial, arrived)
    stats = lax.all_gather(stats, TENSOR, axis=0)
    target, product = finish(stats, summed, arrived, mask, pred, pred_far, hidden_rows)

    product = lax.all_to_all(product.reshape(4, -1, width), "x", 0, 0, tiled=True)
    product = jnp.sum(product.astype(jnp.float32), axis=0).astype(jnp.bfloat16)
    product = lax.all_to_all(product.reshape(8, -1, width), ("h", "y"), 0, 0, tiled=True)
    grad_scale = 1.0 / math.sqrt(MASKS * CLIPS * MASKED)
    pred_grad = jnp.sum(product.astype(jnp.float32), axis=0) * grad_scale
    return (target, pred_grad)


def solution(mesh):
    fine = Mesh(mesh.devices.reshape(2, 4, 4, 2, 4, 2), SEQ + TENSOR)
    placed = (
        P(SEQ, TENSOR),
        P(SEQ, TENSOR),
        P(SEQ, TENSOR),
        P(SEQ, TENSOR),
        P(SEQ, TENSOR),
        P(None, SEQ, None),
        P(None, TENSOR),
        P(None, SEQ),
    )
    return jax.shard_map(
        body,
        mesh=fine,
        in_specs=placed,
        out_specs=(P(SEQ, TENSOR), P(SEQ, TENSOR)),
        check_vma=False,
    )
```

```python
import math

import jax
import jax.numpy as jnp
from jax import lax
from jax.experimental import pallas as pl
from jax.experimental.pallas import tpu as pltpu
from jax.sharding import Mesh
from jax.sharding import PartitionSpec as P

D = 6144
HD = 128
CLIPS = 2
MASKS = 2
MASKED = 3072
HEADS_HERE = 3
SEQ = ("h", "y", "x", "z")
TENSOR = ("w", "c")
LOG2E_ROOT = math.log2(math.e) / math.sqrt(HD)
LEVEL_ROWS = 16
MARK_ROWS = 16
VMEM = pl.BlockSpec(memory_space=pltpu.VMEM)
SMEM = pl.BlockSpec(memory_space=pltpu.SMEM)
ROOMY = pltpu.CompilerParams(vmem_limit_bytes=40 * 1024 * 1024)


def ring(size, distance):
    return [(source, (source + distance) % size) for source in range(size)]


def neighbour(array):
    return lax.ppermute(array, "z", ring(2, 1))


def diagonal(size):
    rows = lax.broadcasted_iota(jnp.int32, (size, size), 0)
    return rows == lax.broadcasted_iota(jnp.int32, (size, size), 1)


def column_to_row(column):
    return jnp.sum(jnp.where(diagonal(column.shape[0]), column, 0.0), axis=0, keepdims=True)


def row_to_column(row):
    return jnp.sum(jnp.where(diagonal(row.shape[1]), row, 0.0), axis=1, keepdims=True)


def pack_kernel(place, queries, keys, values, weight, one, two, three, four, weights):
    for distance, out in enumerate((one, two, three, four)):
        head = jnp.minimum(place[1] ^ distance, HEADS_HERE - 1)
        columns = pl.ds(pl.multiple_of(head * HD, HD), HD)
        out[0] = keys[:, columns]
        out[1] = values[:, columns]
        out[2] = queries[:, columns]
    for copy in range(weights.shape[0]):
        weights[copy] = weight[...]


def pack(place, queries, keys, values, weight):
    piece = jax.ShapeDtypeStruct((3, queries.shape[0], HD), jnp.bfloat16)
    return pl.pallas_call(
        pack_kernel,
        out_shape=(piece,) * 4 + (jax.ShapeDtypeStruct((8,) + weight.shape, jnp.bfloat16),),
        in_specs=[SMEM] + [VMEM] * 4,
        out_specs=(VMEM,) * 5,
    )(place, queries, keys, values, weight)


def attend_kernel(place, q_own, q_far, kv0, kv1, kv2, kv3, out):
    parts = (kv0, kv1, kv2, kv3)
    keys = jnp.concatenate([p[i, 0] for p in parts for i in range(p.shape[0])], axis=0)
    values = jnp.concatenate([p[i, 1] for p in parts for i in range(p.shape[0])], axis=0)
    for q_ref, side in ((q_own, place[0]), (q_far, 1 - place[0])):
        for block in range(0, q_ref.shape[0], 2):
            query = jnp.concatenate([q_ref[block], q_ref[block + 1]], axis=0)
            scores = lax.dot_general(
                query, keys, (((1,), (1,)), ((), ())), preferred_element_type=jnp.float32
            )
            best = jnp.max(scores, axis=1, keepdims=True)
            exponent = jnp.exp2((scores - best) * LOG2E_ROOT)
            total = jnp.sum(exponent, axis=1, keepdims=True)
            summed = jnp.dot(
                exponent.astype(jnp.bfloat16), values, preferred_element_type=jnp.float32
            )
            summed = (summed / total).astype(jnp.bfloat16)
            level = best * LOG2E_ROOT + jnp.log2(total)
            for half in range(2):
                rows = slice(half * HD, (half + 1) * HD)
                row = column_to_row(level[rows])
                first = row.astype(jnp.bfloat16).astype(jnp.float32)
                second = (row - first).astype(jnp.bfloat16).astype(jnp.float32)
                third = row - first - second
                terms = jnp.concatenate(
                    [first, second, third, jnp.zeros((LEVEL_ROWS - 3, HD), jnp.float32)], axis=0
                )
                chunk = 2 * (place[1] ^ (block + half)) + side
                out[chunk, :HD, :] = summed[rows]
                out[chunk, HD:, :] = terms.astype(jnp.bfloat16)


def attend(place, q_own, q_far, kvs):
    chunks = 2 * q_own.shape[0]
    return pl.pallas_call(
        attend_kernel,
        out_shape=jax.ShapeDtypeStruct((chunks, HD + LEVEL_ROWS, HD), jnp.bfloat16),
        in_specs=[SMEM] + [VMEM] * 6,
        out_specs=VMEM,
        compiler_params=ROOMY,
        cost_estimate=pl.CostEstimate(
            flops=4 * 1024 * 2048 * HD, bytes_accessed=2**21, transcendentals=1024 * 2048
        ),
    )(place, q_own, q_far, *kvs)


def combine_kernel(place, chunks, kept, sent):
    heads = []
    for head in range(HEADS_HERE):
        levels = []
        for part in range(2):
            terms = chunks[2 * head + part, HD:, :].astype(jnp.float32)
            levels.append(row_to_column(terms[0:1] + terms[1:2] + terms[2:3]))
        best = jnp.maximum(levels[0], levels[1])
        weights = [jnp.exp2(level - best) for level in levels]
        summed = sum(
            weights[part] * chunks[2 * head + part, :HD, :].astype(jnp.float32) for part in range(2)
        )
        heads.append(summed / (weights[0] + weights[1]))
    columns = jnp.concatenate(heads, axis=1)
    halves = []
    for z in range(2):
        blocks = [columns[:, 96 * x + 48 * z : 96 * x + 48 * z + 48] for x in range(4)]
        half = None
        for x in range(4):
            turned = jnp.concatenate(blocks[x:] + blocks[:x], axis=1)
            half = turned if half is None else jnp.where(place[2] == x, turned, half)
        halves.append(half)
    first = place[0] == 0
    kept[...] = jnp.where(first, halves[0], halves[1]).astype(jnp.bfloat16)
    sent[...] = jnp.where(first, halves[1], halves[0]).astype(jnp.bfloat16)


def combine(place, chunks):
    shape = jax.ShapeDtypeStruct((HD, HEADS_HERE * HD // 2), jnp.bfloat16)
    return pl.pallas_call(
        combine_kernel,
        out_shape=(shape, shape),
        in_specs=[SMEM, VMEM],
        out_specs=(VMEM, VMEM),
    )(place, chunks)


def marks_kernel(mask, marks):
    marks[...] = mask[...].astype(jnp.float32)


def as_marks(mask):
    return pl.pallas_call(
        marks_kernel,
        out_shape=jax.ShapeDtypeStruct(mask.shape, jnp.float32),
        in_specs=[VMEM],
        out_specs=VMEM,
        cost_estimate=pl.CostEstimate(flops=2**29, bytes_accessed=2**21, transcendentals=0),
    )(mask)


def project_kernel(columns, residual, mask, one, two, three, four, partial, sent):
    pieces, tokens, width = columns.shape
    half = width // 2
    total = jnp.concatenate([residual[...].astype(jnp.float32), jnp.zeros(residual.shape, jnp.float32)], axis=0)
    for piece in range(pieces):
        left = jnp.concatenate([columns[piece, :, :half], columns[piece, :, half:]], axis=0)
        right = jnp.concatenate([ref[piece] for ref in (one, two, three, four)], axis=0)
        total += jnp.dot(left, right, preferred_element_type=jnp.float32)
    partial[...] = total
    sent[: 2 * tokens, :] = total.astype(jnp.bfloat16)
    marks = jnp.concatenate([mask[...], jnp.zeros((sent.shape[0] - 2 * tokens - MASKS, tokens), jnp.float32)], axis=0)
    sent[2 * tokens :, :] = jnp.concatenate([marks] * (sent.shape[1] // tokens), axis=1).astype(jnp.bfloat16)


def project(columns, residual, mask, weights):
    pieces, tokens, _ = columns.shape
    rows, width = weights[0].shape[1:]
    count = 4 * pieces * rows * width
    return pl.pallas_call(
        project_kernel,
        out_shape=(
            jax.ShapeDtypeStruct((2 * tokens, width), jnp.float32),
            jax.ShapeDtypeStruct((2 * tokens + MARK_ROWS, width), jnp.bfloat16),
        ),
        in_specs=[VMEM] * 7,
        out_specs=(VMEM, VMEM),
        compiler_params=ROOMY,
        cost_estimate=pl.CostEstimate(
            flops=4 * tokens * count, bytes_accessed=2 * count, transcendentals=0
        ),
    )(columns, residual, mask, *weights)


def add_kernel(partial, arrived, summed, stats):
    tokens = partial.shape[0] // 2
    for side in range(2):
        rows = slice(side * tokens, (side + 1) * tokens)
        other = slice((1 - side) * tokens, (2 - side) * tokens)
        total = partial[rows, :] + arrived[other, :].astype(jnp.float32)
        summed[rows, :] = total
        mean = jnp.sum(total, axis=1, keepdims=True) / total.shape[1]
        off = total - mean
        square = column_to_row(jnp.sum(off * off, axis=1, keepdims=True))
        for copy in range(stats.shape[0]):
            stats[copy, 2 * side : 2 * side + 1, :] = column_to_row(mean)
            stats[copy, 2 * side + 1 : 2 * side + 2, :] = square


def add_up(partial, arrived):
    rows, width = partial.shape
    return pl.pallas_call(
        add_kernel,
        out_shape=(
            jax.ShapeDtypeStruct((rows, width), jnp.float32),
            jax.ShapeDtypeStruct((8, 4, rows // 2), jnp.float32),
        ),
        in_specs=[VMEM] * 2,
        out_specs=(VMEM, VMEM),
        compiler_params=ROOMY,
    )(partial, arrived)


def finish_kernel(stats, summed, arrived, mask, pred, pred_far, hidden, target, product):
    rows_here, width = summed.shape
    tokens = rows_here // 2
    errors = []
    for side, prediction in enumerate((pred, pred_far)):
        rows = slice(side * tokens, (side + 1) * tokens)
        means = stats[:, 2 * side, :]
        mean = jnp.sum(means, axis=0, keepdims=True) * (width / D)
        shift = means - mean
        var = jnp.sum(stats[:, 2 * side + 1, :] + width * shift * shift, axis=0, keepdims=True) / D
        scale = row_to_column(lax.rsqrt(var + 1e-06))
        value = ((summed[rows, :] - row_to_column(mean)) * scale).astype(jnp.bfloat16)
        if side == 0:
            target[...] = value
        value = value.astype(jnp.float32)
        for k in range(MASKS):
            if side == 0:
                marks = mask[k : k + 1, :]
            else:
                marks = arrived[rows_here + k : rows_here + k + 1, :tokens].astype(jnp.float32)
            difference = jnp.clip(prediction[k * tokens : (k + 1) * tokens, :] - value, -1.0, 1.0)
            errors.append((difference * row_to_column(marks)).astype(jnp.bfloat16))
    error = jnp.concatenate(errors, axis=0)
    step = 256
    for start in range(0, hidden.shape[0], step):
        product[start : start + step, :] = jnp.dot(
            hidden[start : start + step, :], error, preferred_element_type=jnp.float32
        ).astype(jnp.bfloat16)


def finish(stats, summed, arrived, mask, pred, pred_far, hidden):
    rows, width = summed.shape
    return pl.pallas_call(
        finish_kernel,
        out_shape=(
            jax.ShapeDtypeStruct((rows // 2, width), jnp.bfloat16),
            jax.ShapeDtypeStruct((hidden.shape[0], width), jnp.bfloat16),
        ),
        in_specs=[VMEM] * 7,
        out_specs=(VMEM, VMEM),
        compiler_params=ROOMY,
        cost_estimate=pl.CostEstimate(
            flops=2 * hidden.shape[0] * hidden.shape[1] * width,
            bytes_accessed=2**22,
            transcendentals=0,
        ),
    )(stats, summed, arrived, mask, pred, pred_far, hidden)


def body(queries, keys, values, residual, out_weight, pred_hidden, pred_weight, mask):
    place = jnp.stack(
        [lax.axis_index(name) for name in ("z", "y", "x")]
    ).astype(jnp.int32)
    *pieces, weight = pack(place, queries, keys, values, out_weight)
    for distance in (1, 2, 3):
        pairs = [(i, i ^ distance) for i in range(4) if i ^ distance < HEADS_HERE]
        pieces[distance] = lax.ppermute(pieces[distance], "y", pairs)
    pieces[1], weight = lax.optimization_barrier((pieces[1], weight))
    kv_own = jnp.stack([piece[:2] for piece in pieces])
    q_own = jnp.stack([piece[2] for piece in pieces])

    width = out_weight.shape[1]
    weight = lax.all_to_all(weight, ("h", "y"), 0, 0, tiled=True)

    kvs = [kv_own] + [lax.ppermute(kv_own, "x", ring(4, d)) for d in (2, 1, 3)]
    q_far = neighbour(q_own)
    kvs, q_far, weight = lax.optimization_barrier((kvs, q_far, weight))
    parts = attend(place, q_own, q_far, kvs)

    hidden = pred_hidden.reshape(-1, pred_hidden.shape[2])
    hidden_far = neighbour(hidden)
    mask, parts = lax.optimization_barrier((mask, parts))
    marks = as_marks(mask)
    weight, marks = lax.optimization_barrier((weight, marks))
    weights = [weight] + [lax.ppermute(weight, "x", ring(4, -d)) for d in (1, 2, 3)]

    parts = lax.all_to_all(parts, ("y", "z"), 0, 0, tiled=True)
    parts, hidden_far = lax.optimization_barrier((parts, hidden_far))
    kept, sent = combine(place, parts)
    attended = jnp.concatenate((kept, neighbour(sent)), axis=1)
    attended = lax.all_gather(attended, "w", axis=0)
    attended = lax.all_gather(attended, "c", axis=1).reshape((8,) + attended.shape[1:])

    partial, sent = project(attended, residual, marks, weights)
    arrived = neighbour(sent)
    hidden, hidden_far, sent = lax.optimization_barrier((hidden, hidden_far, sent))
    pred = jnp.dot(hidden, pred_weight, preferred_element_type=jnp.float32)
    pred_far = jnp.dot(hidden_far, pred_weight, preferred_element_type=jnp.float32)
    z = lax.axis_index("z")
    hidden_rows = [
        lax.dynamic_index_in_dim(h.T.reshape(8, 4, 2, 16, -1), z, 2, keepdims=False)
        for h in (hidden, hidden_far)
    ]
    hidden_rows = jnp.concatenate(hidden_rows, axis=3).transpose(1, 0, 2, 3)
    hidden_rows = hidden_rows.reshape(-1, 2 * hidden.shape[0])

    summed, stats = add_up(partial, arrived)
    stats, pred, pred_far, hidden_rows = lax.optimization_barrier(
        (stats, pred, pred_far, hidden_rows)
    )
    stats = lax.all_to_all(stats, TENSOR, 0, 0, tiled=True)
    target, product = finish(stats, summed, arrived, marks, pred, pred_far, hidden_rows)

    product = lax.all_to_all(product.reshape(4, -1, width), "x", 0, 0, tiled=True)
    product = jnp.sum(product.astype(jnp.float32), axis=0).astype(jnp.bfloat16)
    product = lax.all_to_all(product.reshape(8, -1, width), ("h", "y"), 0, 0, tiled=True)
    grad_scale = 1.0 / math.sqrt(MASKS * CLIPS * MASKED)
    pred_grad = jnp.sum(product.astype(jnp.float32), axis=0) * grad_scale
    return (target, pred_grad)


def solution(mesh):
    fine = Mesh(mesh.devices.reshape(2, 4, 4, 2, 4, 2), SEQ + TENSOR)
    placed = (
        P(SEQ, TENSOR),
        P(SEQ, TENSOR),
        P(SEQ, TENSOR),
        P(SEQ, TENSOR),
        P(SEQ, TENSOR),
        P(None, SEQ, None),
        P(None, TENSOR),
        P(None, SEQ),
    )
    return jax.shard_map(
        body,
        mesh=fine,
        in_specs=placed,
        out_specs=(P(SEQ, TENSOR), P(SEQ, TENSOR)),
        check_vma=False,
    )
```

```python
import math

import jax
import jax.numpy as jnp
from jax import lax
from jax.experimental import pallas as pl
from jax.experimental.pallas import tpu as pltpu
from jax.sharding import Mesh
from jax.sharding import PartitionSpec as P

D = 6144
HD = 128
CLIPS = 2
MASKS = 2
MASKED = 3072
HEADS_HERE = 3
SEQ = ("h", "y", "x", "z")
TENSOR = ("w", "c")
LOG2E_ROOT = math.log2(math.e) / math.sqrt(HD)
LEVEL_ROWS = 16
MARK_ROWS = 16
VMEM = pl.BlockSpec(memory_space=pltpu.VMEM)
SMEM = pl.BlockSpec(memory_space=pltpu.SMEM)
ROOMY = pltpu.CompilerParams(vmem_limit_bytes=40 * 1024 * 1024)


def ring(size, distance):
    return [(source, (source + distance) % size) for source in range(size)]


def neighbour(array):
    return lax.ppermute(array, "z", ring(2, 1))


def diagonal(size):
    rows = lax.broadcasted_iota(jnp.int32, (size, size), 0)
    return rows == lax.broadcasted_iota(jnp.int32, (size, size), 1)


def column_to_row(column):
    return jnp.sum(jnp.where(diagonal(column.shape[0]), column, 0.0), axis=0, keepdims=True)


def row_to_column(row):
    return jnp.sum(jnp.where(diagonal(row.shape[1]), row, 0.0), axis=1, keepdims=True)


def pack_kernel(place, queries, keys, values, weight, one, two, three, four, weights):
    for distance, out in enumerate((one, two, three, four)):
        head = jnp.minimum(place[1] ^ distance, HEADS_HERE - 1)
        columns = pl.ds(pl.multiple_of(head * HD, HD), HD)
        out[0] = keys[:, columns]
        out[1] = values[:, columns]
        out[2] = queries[:, columns]
    for copy in range(weights.shape[0]):
        weights[copy] = weight[...]


def pack(place, queries, keys, values, weight):
    piece = jax.ShapeDtypeStruct((3, queries.shape[0], HD), jnp.bfloat16)
    return pl.pallas_call(
        pack_kernel,
        out_shape=(piece,) * 4 + (jax.ShapeDtypeStruct((8,) + weight.shape, jnp.bfloat16),),
        in_specs=[SMEM] + [VMEM] * 4,
        out_specs=(VMEM,) * 5,
    )(place, queries, keys, values, weight)


def attend_kernel(place, q_own, q_far, kv0, kv1, kv2, kv3, out):
    parts = (kv0, kv1, kv2, kv3)
    keys = jnp.concatenate([p[i, 0] for p in parts for i in range(p.shape[0])], axis=0)
    values = jnp.concatenate([p[i, 1] for p in parts for i in range(p.shape[0])], axis=0)
    for q_ref, side in ((q_own, place[0]), (q_far, 1 - place[0])):
        for block in range(0, q_ref.shape[0], 2):
            query = jnp.concatenate([q_ref[block], q_ref[block + 1]], axis=0)
            scores = lax.dot_general(
                query, keys, (((1,), (1,)), ((), ())), preferred_element_type=jnp.float32
            )
            best = jnp.max(scores, axis=1, keepdims=True)
            exponent = jnp.exp2((scores - best) * LOG2E_ROOT)
            total = jnp.sum(exponent, axis=1, keepdims=True)
            summed = jnp.dot(
                exponent.astype(jnp.bfloat16), values, preferred_element_type=jnp.float32
            )
            summed = (summed / total).astype(jnp.bfloat16)
            level = best * LOG2E_ROOT + jnp.log2(total)
            for half in range(2):
                rows = slice(half * HD, (half + 1) * HD)
                row = column_to_row(level[rows])
                first = row.astype(jnp.bfloat16).astype(jnp.float32)
                second = (row - first).astype(jnp.bfloat16).astype(jnp.float32)
                third = row - first - second
                terms = jnp.concatenate(
                    [first, second, third, jnp.zeros((LEVEL_ROWS - 3, HD), jnp.float32)], axis=0
                )
                chunk = 2 * (place[1] ^ (block + half)) + side
                out[chunk, :HD, :] = summed[rows]
                out[chunk, HD:, :] = terms.astype(jnp.bfloat16)


def attend(place, q_own, q_far, kvs):
    chunks = 2 * q_own.shape[0]
    return pl.pallas_call(
        attend_kernel,
        out_shape=jax.ShapeDtypeStruct((chunks, HD + LEVEL_ROWS, HD), jnp.bfloat16),
        in_specs=[SMEM] + [VMEM] * 6,
        out_specs=VMEM,
        compiler_params=ROOMY,
        cost_estimate=pl.CostEstimate(
            flops=4 * 1024 * 2048 * HD, bytes_accessed=2**21, transcendentals=1024 * 2048
        ),
    )(place, q_own, q_far, *kvs)


def combine_kernel(place, chunks, kept, sent):
    heads = []
    for head in range(HEADS_HERE):
        levels = []
        for part in range(2):
            terms = chunks[2 * head + part, HD:, :].astype(jnp.float32)
            levels.append(row_to_column(terms[0:1] + terms[1:2] + terms[2:3]))
        best = jnp.maximum(levels[0], levels[1])
        weights = [jnp.exp2(level - best) for level in levels]
        summed = sum(
            weights[part] * chunks[2 * head + part, :HD, :].astype(jnp.float32) for part in range(2)
        )
        heads.append(summed / (weights[0] + weights[1]))
    columns = jnp.concatenate(heads, axis=1)
    halves = []
    for z in range(2):
        blocks = [columns[:, 96 * x + 48 * z : 96 * x + 48 * z + 48] for x in range(4)]
        half = None
        for x in range(4):
            turned = jnp.concatenate(blocks[x:] + blocks[:x], axis=1)
            half = turned if half is None else jnp.where(place[2] == x, turned, half)
        halves.append(half)
    first = place[0] == 0
    kept[...] = jnp.where(first, halves[0], halves[1]).astype(jnp.bfloat16)
    sent[...] = jnp.where(first, halves[1], halves[0]).astype(jnp.bfloat16)


def combine(place, chunks):
    shape = jax.ShapeDtypeStruct((HD, HEADS_HERE * HD // 2), jnp.bfloat16)
    return pl.pallas_call(
        combine_kernel,
        out_shape=(shape, shape),
        in_specs=[SMEM, VMEM],
        out_specs=(VMEM, VMEM),
    )(place, chunks)


def marks_kernel(mask, marks):
    marks[...] = mask[...].astype(jnp.float32)


def as_marks(mask):
    return pl.pallas_call(
        marks_kernel,
        out_shape=jax.ShapeDtypeStruct(mask.shape, jnp.float32),
        in_specs=[VMEM],
        out_specs=VMEM,
        cost_estimate=pl.CostEstimate(flops=2**29, bytes_accessed=2**21, transcendentals=0),
    )(mask)


def project_kernel(columns, residual, mask, one, two, three, four, partial, sent):
    pieces, tokens, width = columns.shape
    half = width // 2
    total = jnp.concatenate([residual[...].astype(jnp.float32), jnp.zeros(residual.shape, jnp.float32)], axis=0)
    for piece in range(pieces):
        left = jnp.concatenate([columns[piece, :, :half], columns[piece, :, half:]], axis=0)
        right = jnp.concatenate([ref[piece] for ref in (one, two, three, four)], axis=0)
        total += jnp.dot(left, right, preferred_element_type=jnp.float32)
    partial[...] = total
    sent[: 2 * tokens, :] = total.astype(jnp.bfloat16)
    marks = jnp.concatenate([mask[...], jnp.zeros((sent.shape[0] - 2 * tokens - MASKS, tokens), jnp.float32)], axis=0)
    sent[2 * tokens :, :] = jnp.concatenate([marks] * (sent.shape[1] // tokens), axis=1).astype(jnp.bfloat16)


def project(columns, residual, mask, weights):
    pieces, tokens, _ = columns.shape
    rows, width = weights[0].shape[1:]
    count = 4 * pieces * rows * width
    return pl.pallas_call(
        project_kernel,
        out_shape=(
            jax.ShapeDtypeStruct((2 * tokens, width), jnp.float32),
            jax.ShapeDtypeStruct((2 * tokens + MARK_ROWS, width), jnp.bfloat16),
        ),
        in_specs=[VMEM] * 7,
        out_specs=(VMEM, VMEM),
        compiler_params=ROOMY,
        cost_estimate=pl.CostEstimate(
            flops=4 * tokens * count, bytes_accessed=2 * count, transcendentals=0
        ),
    )(columns, residual, mask, *weights)


def add_kernel(partial, arrived, summed, stats):
    tokens = partial.shape[0] // 2
    for side in range(2):
        rows = slice(side * tokens, (side + 1) * tokens)
        other = slice((1 - side) * tokens, (2 - side) * tokens)
        total = partial[rows, :] + arrived[other, :].astype(jnp.float32)
        summed[rows, :] = total
        mean = jnp.sum(total, axis=1, keepdims=True) / total.shape[1]
        off = total - mean
        square = column_to_row(jnp.sum(off * off, axis=1, keepdims=True))
        for copy in range(stats.shape[0]):
            stats[copy, 2 * side : 2 * side + 1, :] = column_to_row(mean)
            stats[copy, 2 * side + 1 : 2 * side + 2, :] = square


def add_up(partial, arrived):
    rows, width = partial.shape
    return pl.pallas_call(
        add_kernel,
        out_shape=(
            jax.ShapeDtypeStruct((rows, width), jnp.float32),
            jax.ShapeDtypeStruct((8, 4, rows // 2), jnp.float32),
        ),
        in_specs=[VMEM] * 2,
        out_specs=(VMEM, VMEM),
        compiler_params=ROOMY,
    )(partial, arrived)


def finish_kernel(stats, summed, arrived, mask, pred, pred_far, hidden, target, product):
    rows_here, width = summed.shape
    tokens = rows_here // 2
    errors = []
    for side, prediction in enumerate((pred, pred_far)):
        rows = slice(side * tokens, (side + 1) * tokens)
        means = stats[:, 2 * side, :]
        mean = jnp.sum(means, axis=0, keepdims=True) * (width / D)
        shift = means - mean
        var = jnp.sum(stats[:, 2 * side + 1, :] + width * shift * shift, axis=0, keepdims=True) / D
        scale = row_to_column(lax.rsqrt(var + 1e-06))
        value = ((summed[rows, :] - row_to_column(mean)) * scale).astype(jnp.bfloat16)
        if side == 0:
            target[...] = value
        value = value.astype(jnp.float32)
        for k in range(MASKS):
            if side == 0:
                marks = mask[k : k + 1, :]
            else:
                marks = arrived[rows_here:, :tokens].astype(jnp.float32)[k : k + 1]
            difference = jnp.clip(prediction[k * tokens : (k + 1) * tokens, :] - value, -1.0, 1.0)
            errors.append((difference * row_to_column(marks)).astype(jnp.bfloat16))
    error = jnp.concatenate(errors, axis=0)
    step = 256
    for start in range(0, hidden.shape[0], step):
        product[start : start + step, :] = jnp.dot(
            hidden[start : start + step, :], error, preferred_element_type=jnp.float32
        ).astype(jnp.bfloat16)


def finish(stats, summed, arrived, mask, pred, pred_far, hidden):
    rows, width = summed.shape
    return pl.pallas_call(
        finish_kernel,
        out_shape=(
            jax.ShapeDtypeStruct((rows // 2, width), jnp.bfloat16),
            jax.ShapeDtypeStruct((hidden.shape[0], width), jnp.bfloat16),
        ),
        in_specs=[VMEM] * 7,
        out_specs=(VMEM, VMEM),
        compiler_params=ROOMY,
        cost_estimate=pl.CostEstimate(
            flops=2 * hidden.shape[0] * hidden.shape[1] * width,
            bytes_accessed=2**22,
            transcendentals=0,
        ),
    )(stats, summed, arrived, mask, pred, pred_far, hidden)


def body(queries, keys, values, residual, out_weight, pred_hidden, pred_weight, mask):
    place = jnp.stack(
        [lax.axis_index(name) for name in ("z", "y", "x")]
    ).astype(jnp.int32)
    *pieces, weight = pack(place, queries, keys, values, out_weight)
    for distance in (1, 2, 3):
        pairs = [(i, i ^ distance) for i in range(4) if i ^ distance < HEADS_HERE]
        pieces[distance] = lax.ppermute(pieces[distance], "y", pairs)
    pieces[1], weight = lax.optimization_barrier((pieces[1], weight))
    kv_own = jnp.stack([piece[:2] for piece in pieces])
    q_own = jnp.stack([piece[2] for piece in pieces])

    width = out_weight.shape[1]
    weight = lax.all_to_all(weight, ("h", "y"), 0, 0, tiled=True)

    kvs = [kv_own] + [lax.ppermute(kv_own, "x", ring(4, d)) for d in (2, 1, 3)]
    q_far = neighbour(q_own)
    kvs, q_far, weight = lax.optimization_barrier((kvs, q_far, weight))
    parts = attend(place, q_own, q_far, kvs)

    hidden = pred_hidden.reshape(-1, pred_hidden.shape[2])
    hidden_far = neighbour(hidden)
    mask, parts = lax.optimization_barrier((mask, parts))
    marks = as_marks(mask)
    weight, marks = lax.optimization_barrier((weight, marks))
    weights = [weight] + [lax.ppermute(weight, "x", ring(4, -d)) for d in (1, 2, 3)]

    parts = lax.all_to_all(parts, ("y", "z"), 0, 0, tiled=True)
    parts, hidden_far = lax.optimization_barrier((parts, hidden_far))
    kept, sent = combine(place, parts)
    attended = jnp.concatenate((kept, neighbour(sent)), axis=1)
    attended = lax.all_gather(attended, "w", axis=0)
    attended = lax.all_gather(attended, "c", axis=1).reshape((8,) + attended.shape[1:])

    partial, sent = project(attended, residual, marks, weights)
    arrived = neighbour(sent)
    hidden, hidden_far, sent = lax.optimization_barrier((hidden, hidden_far, sent))
    pred = jnp.dot(hidden, pred_weight, preferred_element_type=jnp.float32)
    pred_far = jnp.dot(hidden_far, pred_weight, preferred_element_type=jnp.float32)
    z = lax.axis_index("z")
    hidden_rows = [
        lax.dynamic_index_in_dim(h.T.reshape(8, 4, 2, 16, -1), z, 2, keepdims=False)
        for h in (hidden, hidden_far)
    ]
    hidden_rows = jnp.concatenate(hidden_rows, axis=3).transpose(1, 0, 2, 3)
    hidden_rows = hidden_rows.reshape(-1, 2 * hidden.shape[0])

    summed, stats = add_up(partial, arrived)
    stats, pred, pred_far, hidden_rows = lax.optimization_barrier(
        (stats, pred, pred_far, hidden_rows)
    )
    stats = lax.all_to_all(stats, TENSOR, 0, 0, tiled=True)
    target, product = finish(stats, summed, arrived, marks, pred, pred_far, hidden_rows)

    product = lax.all_to_all(product.reshape(4, -1, width), "x", 0, 0, tiled=True)
    product = jnp.sum(product.astype(jnp.float32), axis=0).astype(jnp.bfloat16)
    product = lax.all_to_all(product.reshape(8, -1, width), ("h", "y"), 0, 0, tiled=True)
    grad_scale = 1.0 / math.sqrt(MASKS * CLIPS * MASKED)
    pred_grad = jnp.sum(product.astype(jnp.float32), axis=0) * grad_scale
    return (target, pred_grad)


def solution(mesh):
    fine = Mesh(mesh.devices.reshape(2, 4, 4, 2, 4, 2), SEQ + TENSOR)
    placed = (
        P(SEQ, TENSOR),
        P(SEQ, TENSOR),
        P(SEQ, TENSOR),
        P(SEQ, TENSOR),
        P(SEQ, TENSOR),
        P(None, SEQ, None),
        P(None, TENSOR),
        P(None, SEQ),
    )
    return jax.shard_map(
        body,
        mesh=fine,
        in_specs=placed,
        out_specs=(P(SEQ, TENSOR), P(SEQ, TENSOR)),
        check_vma=False,
    )
```
